256 devices in a mesh: leaf: 4 (over y), row: 16 (over z, x_lo), col: 4 (over x_hi, core).
Axes of the slice: x: 4 (x_hi: 2, x_lo: 2; x = x_hi * 2 + x_lo), y: 4, z: 8, core: 2. Of those that a mesh axis runs over, the one named last changes fastest.
Arguments:
- rhs_top: float32 [8192, 64], P(('leaf', 'row')), may hold values from -6 to 6
- rhs_mid: float32 [8192, 64], P(('leaf', 'row')), may hold values from -6 to 6
- rhs_low: float32 [8192, 64], P(('leaf', 'row')), may hold values from -6 to 6
- inverse_top: float32 [8192, 8192], P(('leaf', 'row'), 'col'), as said below
- inverse_mid: float32 [8192, 4096], P(('leaf', 'row'), 'col'), as said below
- inverse_low: float32 [8192, 2048], P(('leaf', 'row'), 'col'), as said below
- tiles_mid: float32 [4, 16, 4, 4, 128, 128], P('leaf', 'row', 'col'), may hold values from -0.25 to 0.25
- places_mid: int32 [4, 16, 4, 4], P('leaf', 'row', 'col'), may hold values from 0 to 15, as said below
- tiles_low: float32 [4, 16, 4, 2, 128, 128], P('leaf', 'row', 'col'), may hold values from -0.375 to 0.375
- places_low: int32 [4, 16, 4, 2], P('leaf', 'row', 'col'), may hold values from 0 to 7, as said below
Outputs:
- solved_top: float32 [8192, 64], P(('leaf', 'row'))
- solved_mid: float32 [8192, 64], P(('leaf', 'row'))
- solved_low: float32 [8192, 64], P(('leaf', 'row'))
The draws below stay inside these ranges and needn't reach their ends.
Inputs may be any that keep to these rules, and one draw needn't show every extreme that they name: `places_mid`: within one device the 4 positions are distinct, a quarter of the device's (16) x (1) tile slots. `places_low`: within one device the 2 positions are distinct, a quarter of the device's (8) x (1) tile slots. `inverse_top`: each separator's square block is lower triangular with positive diagonal. `inverse_mid`: each separator's square block is lower triangular with positive diagonal. `inverse_low`: each separator's square block is lower triangular with positive diagonal.
All inputs are finite; a program needn't handle non-finite values.
Results may differ from the reference program's by a relative error of at most 0.00014.
Values sent between devices are 32-bit elements; how exact they have to be, the bound alone decides.
A program may use at most 64 MiB of HBM per device.

```python
import jax
import jax.numpy as jnp
from jax import lax

SEP_ROWS = 128
VECTORS = 64
TILE = 128
S0 = 8192
S1 = 4096
S2 = 2048
NT1 = 4
NT2 = 2
N_LEAF = 4
N_ROW = 16
N_COL = 4


def triangle(noise, diagonal, sep_size):
    row_pos = (jnp.arange(S0, dtype=jnp.int32) % sep_size)[:, None]
    col_pos = jnp.arange(sep_size, dtype=jnp.int32)[None, :]
    lower = jnp.where(col_pos < row_pos, noise * (1.0 / sep_size ** 0.5), 0.0)
    return (lower + jnp.where(col_pos == row_pos, diagonal[:, None], 0.0)).astype(jnp.float32)


def inverse_draw(key, sep_size, diag_low, diag_high):
    first_key, second_key = jax.random.split(key)
    noise = jax.random.normal(first_key, (S0, sep_size), jnp.float32)
    diagonal = jnp.exp(jax.random.uniform(second_key, (S0,), jnp.float32, jnp.log(diag_low), jnp.log(diag_high)))
    return triangle(noise, diagonal, sep_size)


def draw_inverse_top(key, part):
    key = jax.random.fold_in(key, 1)
    return inverse_draw(key, S0, 0.5, 2.0)


def draw_inverse_mid(key, part):
    key = jax.random.fold_in(key, 2)
    return inverse_draw(key, S1, 0.5, 2.0)


def draw_inverse_low(key, part):
    key = jax.random.fold_in(key, 3)
    return inverse_draw(key, S2, 0.5, 2.0)


def choose_places(key, positions, chosen_count):
    subkeys = jax.random.split(key, N_LEAF * N_ROW * N_COL)
    chosen = jax.vmap(lambda subkey: jax.random.permutation(subkey, positions)[:chosen_count])(subkeys)
    return chosen.reshape(N_LEAF, N_ROW, N_COL, chosen_count).astype(jnp.int32)


def draw_places_mid(key, part):
    key = jax.random.fold_in(key, 4)
    return choose_places(key, S0 // N_COL // TILE * (SEP_ROWS // TILE), NT1)


def draw_places_low(key, part):
    key = jax.random.fold_in(key, 5)
    return choose_places(key, S1 // N_COL // TILE * (SEP_ROWS // TILE), NT2)


def steps_of(key, dims, pieces, smallest, high):
    level = 1.0
    for dim, blocks in pieces:
        draws = jax.random.uniform(jax.random.fold_in(jax.random.fold_in(key, 6), dim), (blocks,), jnp.float32, smallest / len(pieces), high / len(pieces))
        level = level * jnp.repeat(jnp.exp(draws), dims[dim] // blocks).reshape((-1,) + (1,) * (len(dims) - 1 - dim))
    return level


def centred(own_key, dims, width, limit, cuts=(), kind=jnp.bfloat16):
    entries = jax.random.normal(own_key, dims, jnp.float32) * width
    if len(cuts) > 0:
        entries = steps_of(own_key, dims, cuts, -0.22, 0.18) * entries
    return jnp.clip(entries, min=-limit, max=limit).astype(kind)


def setup_inputs(seed: int = 0) -> dict:
    splits = jax.random.split(jax.random.key(seed), 11)
    rhs_top = centred(splits[0], (S0, VECTORS), 1.0, 6.0, ((0, 64),), jnp.float32)
    rhs_mid = centred(splits[1], (S0, VECTORS), 1.0, 6.0, ((0, 64),), jnp.float32)
    rhs_low = centred(splits[2], (S0, VECTORS), 1.0, 6.0, ((0, 64),), jnp.float32)
    inverse_top = draw_inverse_top(jax.random.fold_in(splits[10], 71), 0)
    inverse_mid = draw_inverse_mid(jax.random.fold_in(splits[10], 71), 0)
    inverse_low = draw_inverse_low(jax.random.fold_in(splits[10], 71), 0)
    tiles_mid = centred(splits[6], (N_LEAF, N_ROW, N_COL, NT1, TILE, TILE), (TILE * NT1) ** -0.5, 0.25, ((0, 4), (1, 16), (2, 4)), jnp.float32)
    places_mid = draw_places_mid(jax.random.fold_in(splits[10], 71), 0)
    tiles_low = centred(splits[8], (N_LEAF, N_ROW, N_COL, NT2, TILE, TILE), (TILE * NT2) ** -0.5, 0.375, ((0, 4), (1, 16), (2, 4)), jnp.float32)
    places_low = draw_places_low(jax.random.fold_in(splits[10], 71), 0)
    return {"rhs_top": rhs_top, "rhs_mid": rhs_mid, "rhs_low": rhs_low, "inverse_top": inverse_top, "inverse_mid": inverse_mid, "inverse_low": inverse_low, "tiles_mid": tiles_mid, "places_mid": places_mid, "tiles_low": tiles_low, "places_low": places_low}


highest = lax.Precision.HIGHEST


def apply_block(inverse, vectors, sep_size, transpose):
    sep_count = inverse.shape[0] // sep_size
    blocks = inverse.reshape(sep_count, sep_size, sep_size)
    stacked = vectors.reshape(sep_count, sep_size, vectors.shape[1])
    if transpose:
        result = jnp.einsum("jba,jbw->jaw", blocks, stacked, precision=highest)
    else:
        result = jnp.einsum("jab,jbw->jaw", blocks, stacked, precision=highest)
    return result.reshape(vectors.shape)


def tile_places(places, sep_size):
    per_row = SEP_ROWS // TILE
    tile_row = places // per_row
    tile_col = places % per_row
    leaf_ids = jnp.arange(N_LEAF, dtype=jnp.int32)[:, None, None, None]
    row_ids = jnp.arange(N_ROW, dtype=jnp.int32)[None, :, None, None]
    col_ids = jnp.arange(N_COL, dtype=jnp.int32)[None, None, :, None]
    block_start = (leaf_ids * N_ROW + row_ids) * SEP_ROWS
    child_rows = block_start + tile_col * TILE
    parent_rows = (block_start // sep_size) * sep_size + col_ids * (sep_size // N_COL) + tile_row * TILE
    return child_rows.astype(jnp.int32), parent_rows.astype(jnp.int32)


def couple_up(tile_set, places, child_vec, sep_size):
    child_rows, parent_rows = tile_places(places, sep_size)
    offsets = jnp.arange(TILE, dtype=jnp.int32)
    picked = child_vec[child_rows[..., None] + offsets]
    product = jnp.einsum("lrcnab,lrcnbw->lrcnaw", tile_set, picked, precision=highest)
    target = (parent_rows[..., None] + offsets).reshape(-1)
    return jnp.zeros_like(child_vec).at[target].add(product.reshape(-1, child_vec.shape[1]))


def couple_down(tile_set, places, parent, sep_size):
    child_rows, parent_rows = tile_places(places, sep_size)
    offsets = jnp.arange(TILE, dtype=jnp.int32)
    picked = parent[parent_rows[..., None] + offsets]
    product = jnp.einsum("lrcnba,lrcnbw->lrcnaw", tile_set, picked, precision=highest)
    target = (child_rows[..., None] + offsets).reshape(-1)
    return jnp.zeros_like(parent).at[target].add(product.reshape(-1, parent.shape[1]))


def reference(rhs_top, rhs_mid, rhs_low, inverse_top, inverse_mid, inverse_low, tiles_mid, places_mid, tiles_low, places_low):
    low_y = apply_block(inverse_low, rhs_low, S2, False)
    mid_y = apply_block(inverse_mid, rhs_mid - couple_up(tiles_low, places_low, low_y, S1), S1, False)
    top_y = apply_block(inverse_top, rhs_top - couple_up(tiles_mid, places_mid, mid_y, S0), S0, False)
    solved_top = apply_block(inverse_top, top_y, S0, True)
    solved_mid = apply_block(inverse_mid, mid_y - couple_down(tiles_mid, places_mid, solved_top, S0), S1, True)
    solved_low = apply_block(inverse_low, low_y - couple_down(tiles_low, places_low, solved_mid, S1), S2, True)
    return (solved_top, solved_mid, solved_low)
```

```python
import functools

import jax
import jax.numpy as jnp
from jax import lax
from jax.experimental import pallas as pl
from jax.experimental.pallas import tpu as pltpu
from jax.sharding import PartitionSpec as P

MESH = pl.DeviceIdType.MESH
TILE = 128
BATCHES = 2
N_LEAF, N_Z, N_X, N_COL = 4, 8, 2, 4
N_ROW = N_Z * N_X
BLOCK = 8
bf16 = jnp.bfloat16
f32 = jnp.float32


def outward(count):
    middle = count // 2
    return [(middle + (-1 if j % 2 else 1) * ((j + 1) // 2)) % count for j in range(count)]


def split(a):
    high = a.astype(bf16)
    return high, (a - high.astype(f32)).astype(bf16)


def product(a, high, low):
    width = a.shape[0]
    a_high, a_low = split(a)
    both = jnp.dot(jnp.concatenate([a_high, a_low], axis=0), high, preferred_element_type=f32)
    return both[:width] + both[width:] + jnp.dot(a_high, low, preferred_element_type=f32)


def kernel(
    rhs_top, rhs_mid, rhs_low, inv_top, inv_mid, inv_low, tiles_mid, places_mid, tiles_low, places_low,
    out_top, out_mid, out_low,
    rt, rm, rl, it, im, il, tm, tl,
    rtt, rmt, rlt,
    top_h, top_l, topt_h, topt_l, mid_h, mid_l, midt_h, midt_l, low_h, low_l, lowt_h, lowt_l,
    tm_h, tm_l, tmt_h, tmt_l, tl_h, tl_l, tlt_h, tlt_l,
    x_low,
    send1, got1, x_mid, send2, got2, x_top, send3, got3, s_top_0, s_top_1, send4, got4, s_mid_0, s_mid_1, send5, got5, tail5,
    col_got, low_y, mid_y,
    o_top, o_mid, o_low,
    load_sem, start_sem, start_out, rs_sem, rs_out, ag_sem, ag_out, col_sem, col_out, res_sem, res_out, end_sem, end_out,
):
    width = 64 // BATCHES
    per_tile = width // BLOCK
    leaf = lax.axis_index("leaf")
    row = lax.axis_index("row")
    col = lax.axis_index("col")
    z = row // N_X
    x = lax.rem(row, N_X)

    rows_at = {}
    for dz in range(N_Z):
        for dx in range(N_X):
            rows_at[dz, dx] = lax.rem(z + dz, N_Z) * N_X + lax.rem(x + dx, N_X)
    pair = leaf // 2 * 2

    def peers(kind):
        if kind == "top":
            leaves = [(lax.rem(leaf + dy, N_LEAF), dy) for dy in outward(N_LEAF)]
        elif kind == "mid":
            leaves = [(pair + lax.rem(leaf - pair + dy, 2), dy) for dy in (1, 0)]
        else:
            leaves = [(leaf, 0)]
        found = []
        for other, dy in leaves:
            for dz in outward(N_Z):
                for dx in (1, 0):
                    if (dy, dz, dx) != (0, 0, 0):
                        r = rows_at[dz, dx]
                        base = {"top": other, "mid": other - pair, "low": 0}[kind]
                        found.append((base * N_ROW + r, (other, r, col)))
        return found

    group = {k: peers(k) for k in ("top", "mid", "low")}
    own = {"top": leaf * N_ROW + row, "mid": (leaf - pair) * N_ROW + row, "low": row}
    others = [(leaf, row, lax.rem(col + d, N_COL)) for d in (2, 3, 1)]

    target_row = col * 4 + row // 4
    source_col = row // 4
    source_row = lax.rem(row, 4) * 4

    def remote(src, dst, send, recv, device):
        return pltpu.make_async_remote_copy(
            src_ref=src, dst_ref=dst, send_sem=send, recv_sem=recv, device_id=device, device_id_type=MESH
        )

    loads = [
        pltpu.make_async_copy(src, dst, load_sem.at[i])
        for i, (src, dst) in enumerate(
            [
                (rhs_low, rl),
                (inv_low, il),
                (tiles_low.at[0, 0, 0], tl),
                (rhs_mid, rm),
                (inv_mid, im),
                (tiles_mid.at[0, 0, 0], tm),
                (rhs_top, rt),
                (inv_top, it),
            ]
        )
    ]
    for load in loads:
        load.start()

    barrier = pltpu.get_barrier_semaphore()
    for _, device in group["top"]:
        pl.semaphore_signal(barrier, inc=1, device_id=device, device_id_type=MESH)
    for device in others:
        pl.semaphore_signal(barrier, inc=1, device_id=device, device_id_type=MESH)
    for i in range(4):
        source = (leaf, source_row + i, source_col)

        @pl.when(jnp.logical_or(source_row + i != row, source_col != col))
        def _():
            pl.semaphore_signal(barrier, inc=1, device_id=source, device_id_type=MESH)

    self_target = (target_row == row).astype(jnp.int32)

    def keep(ref, value):
        for b in range(BATCHES):
            ref[b] = value[b * width : (b + 1) * width].reshape(per_tile, BLOCK, TILE)

    def prepare(raw, high, low, high_t, low_t):
        for p in range(raw.shape[1] // TILE):
            cut = slice(p * TILE, (p + 1) * TILE)
            block = raw[:, cut]
            high[:, cut], low[:, cut] = split(block)
            high_t[cut, :], low_t[cut, :] = split(block.T)

    def prepare_tiles(raw, high, low, high_t, low_t):
        for n in range(raw.shape[0]):
            block = raw[n]
            high[n], low[n] = split(block)
            high_t[n], low_t[n] = split(block.T)

    loads[0].wait()
    keep(rlt, rl[...])
    pl.semaphore_wait(barrier, len(group["top"]) + len(others) + 4 - self_target)

    is_source = col == row // 4
    place_low = lax.rem(row, 4) * per_tile

    @pl.when(is_source)
    def _():
        for b in range(BATCHES):
            here = x_low.at[b, pl.ds(place_low, per_tile)]
            for _, device in group["low"]:
                remote(rlt.at[b], here, start_out.at[b], start_sem.at[b], device).start()
            pltpu.make_async_copy(rlt.at[b], here, start_sem.at[b]).start()

    loads[1].wait()
    prepare(il, low_h, low_l, lowt_h, lowt_l)

    def batch(ref, b):
        return ref[b] if isinstance(ref, tuple) else ref.at[b]

    def whole(ref, sem):
        return pltpu.make_async_copy(ref, ref, sem)

    def columns(ref, b, positions):
        return jnp.concatenate(
            [batch(ref, b)[p * per_tile : (p + 1) * per_tile].reshape(width, TILE) for p in range(positions)],
            axis=1,
        )

    def forward(ref, b, positions, high_t, low_t):
        return product(columns(ref, b, positions), high_t[...], low_t[...])

    def send_col(stage, b, value):
        col_got[stage, b, col] = value
        for device in others:
            mine = col_got.at[stage, b, col]
            remote(mine, mine, col_out.at[stage, b], col_sem.at[stage, b], device).start()

    def get_col(stage, b):
        whole(col_got.at[stage, b, pl.ds(0, N_COL - 1)], col_sem.at[stage, b]).wait()
        got = [col_got[stage, b, c] for c in range(N_COL)]
        return (got[0] + got[1]) + (got[2] + got[3])

    def send_shares(stage, b, kind, send, got):
        me = own[kind]
        for k, device in group[kind]:
            remote(send.at[b, k], got.at[b, me], rs_out.at[stage, b], rs_sem.at[stage, b], device).start()
        got[b, me] = send[b, me]

    def sum_shares(stage, b, kind, got):
        whole(got.at[b, pl.ds(0, len(group[kind]))], rs_sem.at[stage, b]).wait()
        return jnp.sum(got[b], axis=0)

    def spread(stage, b, kind, total, ref):
        mine = batch(ref, b).at[own[kind]]
        mine[...] = total
        for _, device in group[kind]:
            remote(mine, mine, ag_out.at[stage, b], ag_sem.at[stage, b], device).start()

    def get_columns(stage, b, kind, ref):
        whole(batch(ref, b).at[pl.ds(0, len(group[kind]))], ag_sem.at[stage, b]).wait()

    def lift(vector, b, places, high_t, low_t, rhs_t, is_mine, my_place, send, positions):
        rhs = jnp.where(is_mine, rhs_t[b].reshape(width, TILE), 0.0)
        parts = [product(vector, high_t[n], low_t[n]) for n in range(high_t.shape[0])]
        for p in range(positions):
            value = jnp.where(my_place == p, rhs, 0.0)
            for n, part in enumerate(parts):
                value = value - jnp.where(places[0, 0, 0, n] == p, part, 0.0)
            send[b, p * per_tile : (p + 1) * per_tile] = value.reshape(per_tile, BLOCK, TILE)

    def lower(ref, b, places, high, low):
        total = None
        for n in range(high.shape[0]):
            place = places[0, 0, 0, n] * per_tile
            picked = jnp.concatenate([batch(ref, b)[place + q] for q in range(per_tile)], axis=0)
            part = product(picked, high[n], low[n])
            total = part if total is None else total + part
        return total

    def backward(value, b, high, low, send):
        for p in range(high.shape[1] // TILE):
            cut = slice(p * TILE, (p + 1) * TILE)
            part = product(value, high[:, cut], low[:, cut])
            send[b, p * per_tile : (p + 1) * per_tile] = part.reshape(per_tile, BLOCK, TILE)

    mid_index = (leaf - pair) * N_ROW + row
    mine_mid, place_mid = col == mid_index // 8, lax.rem(mid_index, 8)
    mine_top, place_top = col == leaf, row

    def send_result(level, b, ref, mine, place, out):
        @pl.when(mine)
        def _():
            src = batch(ref, b).at[pl.ds(place * per_tile, per_tile)]
            for device in others:
                remote(src, out.at[b], res_out.at[level, b], res_sem.at[level, b], device).start()
            pltpu.make_async_copy(src, out.at[b], res_sem.at[level, b]).start()

    def finish(ref, out):
        out[...] = ref[...].reshape(64, TILE)

    every = range(BATCHES)
    s_top, s_mid = (s_top_0, s_top_1), (s_mid_0, s_mid_1)
    for b in every:
        whole(x_low.at[b], start_sem.at[b]).wait()
        send_col(0, b, forward(x_low, b, 4, lowt_h, lowt_l))
    loads[2].wait()
    prepare_tiles(tl, tl_h, tl_l, tlt_h, tlt_l)
    loads[3].wait()
    keep(rmt, rm[...])
    for b in every:
        low_y[b] = get_col(0, b)
        lift(low_y[b], b, places_low, tlt_h, tlt_l, rmt, mine_mid, place_mid, send1, 8)
        send_shares(0, b, "mid", send1, got1)
    loads[4].wait()
    prepare(im, mid_h, mid_l, midt_h, midt_l)
    for b in every:
        spread(0, b, "mid", sum_shares(0, b, "mid", got1), x_mid)
    loads[5].wait()
    prepare_tiles(tm, tm_h, tm_l, tmt_h, tmt_l)
    loads[6].wait()
    keep(rtt, rt[...])
    for b in every:
        get_columns(0, b, "mid", x_mid)
        send_col(1, b, forward(x_mid, b, 8, midt_h, midt_l))
    for b in every:
        mid_y[b] = get_col(1, b)
        lift(mid_y[b], b, places_mid, tmt_h, tmt_l, rtt, mine_top, place_top, send2, 16)
        send_shares(1, b, "top", send2, got2)
    loads[7].wait()
    prepare(it, top_h, top_l, topt_h, topt_l)
    for b in every:
        spread(1, b, "top", sum_shares(1, b, "top", got2), x_top)
    for b in every:
        get_columns(1, b, "top", x_top)
        send_col(2, b, forward(x_top, b, 16, topt_h, topt_l))
    for b in every:
        backward(get_col(2, b), b, top_h, top_l, send3)
        send_shares(2, b, "top", send3, got3)
    for b in every:
        spread(2, b, "top", sum_shares(2, b, "top", got3), s_top)
    for b in every:
        get_columns(2, b, "top", s_top)
        send_col(3, b, lower(s_top, b, places_mid, tm_h, tm_l))
        send_result(0, b, s_top, mine_top, place_top, o_top)
    for b in every:
        backward(mid_y[b] - get_col(3, b), b, mid_h, mid_l, send4)
        send_shares(3, b, "mid", send4, got4)
    for b in every:
        spread(3, b, "mid", sum_shares(3, b, "mid", got4), s_mid)
    for b in every:
        get_columns(3, b, "mid", s_mid)
        send_col(4, b, lower(s_mid, b, places_low, tl_h, tl_l))
        send_result(1, b, s_mid, mine_mid, place_mid, o_mid)
    for b in every:
        backward(low_y[b] - get_col(4, b), b, low_h, low_l, send5)
        send_shares(4, b, "low", send5, got5)
    slot = lax.rem(row, 4)
    for b in every:
        tail5[b] = sum_shares(4, b, "low", got5)
        for c in range(N_COL):
            to_self = jnp.logical_and(col == c, target_row == row)

            @pl.when(to_self)
            def _():
                pltpu.make_async_copy(tail5.at[b], o_low.at[b, slot], end_sem.at[b]).start()

            @pl.when(jnp.logical_not(to_self))
            def _():
                remote(
                    tail5.at[b], o_low.at[b, slot], end_out.at[b], end_sem.at[b], (leaf, target_row, c)
                ).start()

    for level, (ref, out) in enumerate([(o_top, out_top), (o_mid, out_mid)]):
        for b in every:
            whole(ref.at[b], res_sem.at[level, b]).wait()
        finish(ref, out)
    for b in every:
        whole(o_low.at[b], end_sem.at[b]).wait()
    finish(o_low, out_low)

    for b in every:

        @pl.when(is_source)
        def _():
            for _ in group["low"]:
                whole(rlt.at[b], start_out.at[b]).wait()

        for level, mine in enumerate([mine_top, mine_mid]):

            @pl.when(mine)
            def _():
                for _ in others:
                    whole(o_top.at[b], res_out.at[level, b]).wait()

        for stage, (kind, send, ref) in enumerate(
            [
                ("mid", send1, x_mid),
                ("top", send2, x_top),
                ("top", send3, s_top),
                ("mid", send4, s_mid),
                ("low", send5, None),
            ]
        ):
            count = len(group[kind])
            whole(send.at[b, pl.ds(0, count)], rs_out.at[stage, b]).wait()
            if ref is not None:
                whole(batch(ref, b).at[pl.ds(0, count)], ag_out.at[stage, b]).wait()
            whole(col_got.at[stage, b, pl.ds(0, N_COL - 1)], col_out.at[stage, b]).wait()
        for c in range(N_COL):

            @pl.when(jnp.logical_not(jnp.logical_and(col == c, target_row == row)))
            def _():
                whole(tail5.at[b], end_out.at[b]).wait()


def body(rhs_top, rhs_mid, rhs_low, *others):
    width = 64 // BATCHES
    per_tile = width // BLOCK
    vm = pltpu.VMEM

    def blocks(count):
        return vm((BATCHES, count, BLOCK, TILE), f32)

    def alone(count):
        return vm((count, BLOCK, TILE), f32)

    def halves(*shape):
        return [vm(shape, bf16)] * 2

    rhs = [vm((64, TILE), f32)] * 3
    scratch = rhs + [
        vm((128, 2048), f32), vm((128, 1024), f32), vm((128, 512), f32), vm((4, 128, 128), f32), vm((2, 128, 128), f32),
    ]
    scratch += [blocks(per_tile)] * 3
    for size in (2048, 1024, 512):
        scratch += halves(128, size) + halves(size, 128)
    for count in (4, 2):
        scratch += halves(count, 128, 128) * 2
    scratch += [blocks(4 * per_tile)]
    scratch += [blocks(32)] * 3 + [blocks(64)] * 5 + [alone(64)] * 2 + [blocks(32)] * 2 + [alone(32)] * 2
    scratch += [blocks(16)] * 2 + [vm((BATCHES, BLOCK, TILE), f32)]
    scratch += [vm((5, BATCHES, N_COL, width, TILE), f32)] + [vm((BATCHES, width, TILE), f32)] * 2
    scratch += [blocks(per_tile)] * 3
    dma = pltpu.SemaphoreType.DMA
    scratch += [
        dma((8,)), dma((BATCHES,)), dma((BATCHES,)), dma((5, BATCHES)), dma((5, BATCHES)), dma((4, BATCHES)),
        dma((4, BATCHES)), dma((5, BATCHES)), dma((5, BATCHES)), dma((2, BATCHES)), dma((2, BATCHES)),
        dma((BATCHES,)), dma((BATCHES,)),
    ]
    anywhere = pl.BlockSpec(memory_space=pltpu.HBM)
    scalars = pl.BlockSpec(memory_space=pltpu.SMEM)
    out = pl.BlockSpec(memory_space=pltpu.VMEM)
    solved = pl.pallas_call(
        kernel,
        name="solve",
        out_shape=[jax.ShapeDtypeStruct((64, TILE), f32)] * 3,
        in_specs=[anywhere] * 7 + [scalars, anywhere, scalars],
        out_specs=[out] * 3,
        scratch_shapes=scratch,
        compiler_params=pltpu.CompilerParams(
            collective_id=0, has_side_effects=True, vmem_limit_bytes=60 * 1024 * 1024
        ),
    )(rhs_top.T, rhs_mid.T, rhs_low.T, *others)
    return tuple(part.T for part in solved)


def solution(mesh):
    vector = P(("leaf", "row"), None)
    matrix = P(("leaf", "row"), "col")
    tiles = P("leaf", "row", "col", None, None, None)
    places = P("leaf", "row", "col", None)
    return jax.shard_map(
        body,
        mesh=mesh,
        in_specs=(vector, vector, vector, matrix, matrix, matrix, tiles, places, tiles, places),
        out_specs=(vector, vector, vector),
        check_vma=False,
    )
```

```python
import jax
import jax.numpy as jnp
from jax import lax
from jax.experimental import pallas as pl
from jax.experimental.pallas import tpu as pltpu
from jax.sharding import PartitionSpec as P

MESH = pl.DeviceIdType.MESH
TILE = 128
BATCHES = 2
N_LEAF, N_Z, N_X, N_COL = 4, 8, 2, 4
N_ROW = N_Z * N_X
SHARE = 64 // N_COL
BLOCK = SHARE // BATCHES
bf16 = jnp.bfloat16
f32 = jnp.float32
TOP, MID, LOW = 64, 32, 16
PIECES = 2
NN = (((1,), (0,)), ((), ()))
NT = (((1,), (1,)), ((), ()))


def outward(count):
    middle = count // 2
    return [(middle + (-1 if j % 2 else 1) * ((j + 1) // 2)) % count for j in range(count)]


def split(a):
    high = a.astype(bf16)
    return high, (a - high.astype(f32)).astype(bf16)


def product(a, high, low, dims):
    width = a.shape[0]
    a_high = a.astype(bf16).astype(f32)
    both = jnp.concatenate([a_high, a - a_high], axis=0).astype(bf16)
    one = lax.dot_general(both, high, dims, preferred_element_type=f32)
    two = lax.dot_general(both, low, dims, preferred_element_type=f32)
    return (one[:width] + one[width:]) + (two[:width] + two[width:])


def kernel(
    rhs_top, rhs_mid, rhs_low, inv_top, inv_mid, inv_low, tiles_mid, places_mid, tiles_low, places_low,
    out_top, out_mid, out_low,
    rt, rm, rl, rt_cut, rm_cut, rl_cut,
    it, im, il, tm, tl, all_mid, all_low,
    top_h, top_l, mid_h, mid_l, low_h, low_l, own_mid_h, own_mid_l, own_low_h, own_low_l,
    tm_h, tm_l, tl_h, tl_l, own_tm_h, own_tm_l, own_tl_h, own_tl_l,
    x_low, send1, got1, x_mid, send2, got2, x_top, send3, got3, s_top_0, s_top_1, send4, got4, s_mid_0, s_mid_1,
    send5, got5, tail5, col_got, low_y, mid_y, o_top, o_mid, o_low,
    load_sem, place_sem, place_out, start_sem, start_out, rs_sem, rs_out, ag_sem, ag_out, col_sem, col_out,
    res_sem, res_out, far_sem, far_out, near_sem, near_out, pass_sem, pass_out,
):
    leaf = lax.axis_index("leaf")
    row = lax.axis_index("row")
    col = lax.axis_index("col")
    z = row // N_X
    x = lax.rem(row, N_X)
    pair = leaf // 2 * 2
    every = range(BATCHES)
    wide = N_COL * BLOCK
    s_top, s_mid = (s_top_0, s_top_1), (s_mid_0, s_mid_1)

    rows_at = {}
    for dz in range(N_Z):
        for dx in range(N_X):
            rows_at[dz, dx] = lax.rem(z + dz, N_Z) * N_X + lax.rem(x + dx, N_X)
    row_offsets = [(dz, dx) for dz in outward(N_Z) for dx in (1, 0)]

    def peers(kind):
        if kind == "top":
            leaves = [(lax.rem(leaf + dy, N_LEAF), dy) for dy in outward(N_LEAF)]
        elif kind == "mid":
            leaves = [(pair + lax.rem(leaf - pair + dy, 2), dy) for dy in (1, 0)]
        else:
            leaves = [(leaf, 0)]
        found = []
        for other, dy in leaves:
            for dz, dx in row_offsets:
                if (dy, dz, dx) != (0, 0, 0):
                    r = rows_at[dz, dx]
                    base = {"top": other, "mid": other - pair, "low": 0}[kind]
                    found.append((base * N_ROW + r, (other, r, col)))
        return found

    group = {k: peers(k) for k in ("top", "mid", "low")}
    own = {"top": leaf * N_ROW + row, "mid": (leaf - pair) * N_ROW + row, "low": row}
    other_cols = [lax.rem(col + d, N_COL) for d in (2, 3, 1)]
    others = [(leaf, row, c) for c in other_cols]
    far_col = lax.rem(col + 2, N_COL)
    near_col = col + 1 - 2 * lax.rem(col, 2)
    far, near = (leaf, row, far_col), (leaf, row, near_col)
    on_diagonal = leaf == col

    def remote(src, dst, send, recv, device):
        return pltpu.make_async_remote_copy(
            src_ref=src, dst_ref=dst, send_sem=send, recv_sem=recv, device_id=device, device_id_type=MESH
        )

    def whole(ref, sem):
        return pltpu.make_async_copy(ref, ref, sem)

    def batch(ref, b):
        return ref[b] if isinstance(ref, tuple) else ref.at[b]

    gathered = [
        (tiles_mid.at[0, 0, 0], tm),
        (inv_mid, im),
        (tiles_low.at[0, 0, 0], tl),
        (inv_low, il),
    ]
    places_of = [(inv_low, il.at[col]), (tiles_low.at[0, 0, 0], tl.at[col]), (inv_mid, im.at[col])]
    places_of += [(tiles_mid.at[0, 0, 0], tm.at[col]), (inv_top, it)]
    copies = [(rhs_low, rl), places_of[0], places_of[1], (rhs_mid, rm), places_of[2], places_of[3], (rhs_top, rt)]
    copies += [places_of[4]]
    loads = [pltpu.make_async_copy(src, dst, load_sem.at[i]) for i, (src, dst) in enumerate(copies)]
    for load in loads:
        load.start()

    barrier = pltpu.get_barrier_semaphore()
    for _, device in group["top"]:
        pl.semaphore_signal(barrier, inc=1, device_id=device, device_id_type=MESH)
    for device in others:
        pl.semaphore_signal(barrier, inc=1, device_id=device, device_id_type=MESH)
    for dy in outward(N_LEAF):
        for dz, dx in row_offsets:
            source = (lax.rem(leaf + dy, N_LEAF), rows_at[dz, dx], leaf)
            if (dy, dz, dx) != (0, 0, 0):
                pl.semaphore_signal(barrier, inc=1, device_id=source, device_id_type=MESH)
            else:

                @pl.when(jnp.logical_not(on_diagonal))
                def _():
                    pl.semaphore_signal(barrier, inc=1, device_id=source, device_id_type=MESH)

    def cut_batches(ref, to):
        for b in every:
            for q in range(N_COL):
                to[b, q * BLOCK : (q + 1) * BLOCK] = ref[q * SHARE + b * BLOCK : q * SHARE + (b + 1) * BLOCK]

    loads[0].wait()
    cut_batches(rl, rl_cut)
    pl.semaphore_wait(barrier, len(group["top"]) + len(others) + TOP - on_diagonal.astype(jnp.int32))

    is_source = col == row // 4
    place_low = lax.rem(row, 4)

    @pl.when(is_source)
    def _():
        for b in every:
            here = x_low.at[b, place_low]
            for _, device in group["low"]:
                remote(rl_cut.at[b], here, start_out.at[b], start_sem.at[b], device).start()
            pltpu.make_async_copy(rl_cut.at[b], here, start_sem.at[b]).start()

    pieces = []
    for i, count in ((0, 4), (1, 8), (2, 2), (3, 4)):
        step = gathered[i][0].shape[0] // count
        pieces += [(i, pl.ds(n * step, step)) for n in range(count)]
    pieces.reverse()

    def gather_far(count=PIECES):
        for _ in range(min(count, len(pieces))):
            i, cut = pieces.pop()
            src, dst = gathered[i]
            remote(src.at[cut], dst.at[col, cut], far_out.at[i], far_sem.at[i], far).start()

    def forward_part(i):
        dst = gathered[i][1].at[far_col]
        whole(dst, far_sem.at[i]).wait()
        remote(dst, dst, pass_out.at[i], pass_sem.at[i], near).start()

    def gathered_all(i):
        part = gathered[i][1].at[0]
        whole(part, near_sem.at[i]).wait()
        whole(part, pass_sem.at[i]).wait()

    for (src, dst), sem, out in ((places_low, all_low), place_sem.at[0], place_out.at[0]), (
        (places_mid, all_mid), place_sem.at[1], place_out.at[1]
    ):
        for device in others:
            remote(src, dst.at[col], out, sem, device).start()
        for n in range(src.shape[3]):
            dst[col, 0, 0, 0, n] = src[0, 0, 0, n]
    for i, (src, dst) in enumerate(gathered):
        remote(src, dst.at[col], near_out.at[i], near_sem.at[i], near).start()
    gather_far()

    def prepare(raw, high, low):
        size = raw.shape[2]
        for c in range(N_COL):
            for p in range(0, size, 512):
                cut = slice(c * size + p, c * size + p + 512)
                high[:, cut], low[:, cut] = split(raw[c, :, p : p + 512])

    def prepare_own(raw, high, low):
        for p in range(0, high.shape[1], 512):
            cut = slice(p, p + 512)
            high[:, cut], low[:, cut] = split(raw[:, cut])

    def prepare_tiles(raw, high, low):
        count = raw.shape[1]
        for c in range(N_COL):
            for n in range(count):
                cut = slice((c * count + n) * TILE, (c * count + n + 1) * TILE)
                high[cut], low[cut] = split(raw[c, n])

    def prepare_own_tiles(raw, high, low):
        for n in range(raw.shape[1]):
            cut = slice(n * TILE, (n + 1) * TILE)
            high[cut], low[cut] = split(raw[col, n])

    loads[1].wait()
    prepare_own(il.at[col], own_low_h, own_low_l)

    def send_shares(stage, b, kind, send, got):
        me = own[kind]
        for k, device in group[kind]:
            remote(send.at[b, k], got.at[b, me], rs_out.at[stage, b], rs_sem.at[stage, b], device).start()
        got[b, me] = send[b, me]

    def sum_shares(stage, b, kind, got):
        whole(got.at[b, pl.ds(0, len(group[kind]))], rs_sem.at[stage, b]).wait()
        return jnp.sum(got[b], axis=0)

    def spread(stage, b, kind, total, ref):
        mine = batch(ref, b).at[own[kind]]
        mine[...] = total
        for _, device in group[kind]:
            remote(mine, mine, ag_out.at[stage, b], ag_sem.at[stage, b], device).start()

    def get_columns(stage, b, kind, ref):
        whole(batch(ref, b).at[pl.ds(0, len(group[kind]))], ag_sem.at[stage, b]).wait()

    def send_col(stage, b, value):
        mine = col_got.at[stage, b, col]
        mine[...] = value
        for device in others:
            remote(mine, mine, col_out.at[stage, b], col_sem.at[stage, b], device).start()

    def get_col(stage, b):
        whole(col_got.at[stage, b, pl.ds(0, N_COL - 1)], col_sem.at[stage, b]).wait()
        got = [col_got[stage, b, c] for c in range(N_COL)]
        return (got[0] + got[1]) + (got[2] + got[3])

    def forward(ref, b, positions, high, low):
        columns = jnp.concatenate(
            [ref[b, p * N_COL : (p + 1) * N_COL].reshape(wide, TILE) for p in range(positions)], axis=1
        )
        return product(columns, high[...], low[...], NT)

    def lift(vector, b, places, high, low, rhs, is_mine, my_place, send, positions):
        count = places.shape[3]
        parts = product(vector, high[...], low[...], NT)
        mine = jnp.where(is_mine, rhs[b], 0.0)
        for p in range(positions):
            value = jnp.where(my_place == p, mine, 0.0)
            for n in range(count):
                value = value - jnp.where(places[0, 0, 0, n] == p, parts[:, n * TILE : (n + 1) * TILE], 0.0)
            send[b, p * N_COL : (p + 1) * N_COL] = value.reshape(N_COL, BLOCK, TILE)

    def lower(ref, b, places, high, low, positions):
        count = places.shape[4]
        picked = [
            batch(ref, b)[c * positions + places[c, 0, 0, 0, n]] for c in range(N_COL) for n in range(count)
        ]
        return product(jnp.concatenate(picked, axis=1), high[...], low[...], NN)

    def backward(value, b, high, low, send):
        part = product(value, high[...], low[...], NN)
        for p in range(high.shape[1] // TILE):
            send[b, p] = part[:, p * TILE : (p + 1) * TILE]

    def own_columns(ref, b):
        return ref[b, pl.ds(pl.multiple_of(col * BLOCK, BLOCK), BLOCK)]

    def send_result(level, b, src, out):
        place = pl.ds(pl.multiple_of(col * SHARE + b * BLOCK, BLOCK), BLOCK)
        for device in others:
            remote(src, out.at[place], res_out.at[level, b], res_sem.at[level, b], device).start()
        out[place] = src[...]

    mid_index = own["mid"]
    mine_mid, place_mid = col == mid_index // 8, lax.rem(mid_index, 8)

    for b in every:
        whole(x_low.at[b], start_sem.at[b]).wait()
        columns = jnp.concatenate([x_low[b, p] for p in range(4)], axis=1)
        send_col(0, b, product(columns, own_low_h[...], own_low_l[...], NT))
    gather_far()
    loads[2].wait()
    prepare_own_tiles(tl, own_tl_h, own_tl_l)
    loads[3].wait()
    cut_batches(rm, rm_cut)
    for b in every:
        low_y[b] = get_col(0, b)
        lift(low_y[b], b, places_low, own_tl_h, own_tl_l, rm_cut, mine_mid, place_mid, send1, 8)
        send_shares(0, b, "mid", send1, got1)
    gather_far()
    loads[4].wait()
    prepare_own(im.at[col], own_mid_h, own_mid_l)
    for b in every:
        spread(0, b, "mid", sum_shares(0, b, "mid", got1), x_mid)
    gather_far()
    loads[5].wait()
    prepare_own_tiles(tm, own_tm_h, own_tm_l)
    loads[6].wait()
    cut_batches(rt, rt_cut)
    for b in every:
        get_columns(0, b, "mid", x_mid)
        send_col(1, b, forward(x_mid, b, 8, own_mid_h, own_mid_l))
    gather_far()
    for b in every:
        mid_y[b] = get_col(1, b)
        lift(mid_y[b], b, places_mid, own_tm_h, own_tm_l, rt_cut, on_diagonal, row, send2, 16)
        send_shares(1, b, "top", send2, got2)
    gather_far()
    loads[7].wait()
    prepare_own(it, top_h, top_l)
    for b in every:
        spread(1, b, "top", sum_shares(1, b, "top", got2), x_top)
    gather_far()
    for b in every:
        get_columns(1, b, "top", x_top)
        send_col(2, b, forward(x_top, b, 16, top_h, top_l))
    gather_far()
    for b in every:
        part = product(get_col(2, b), top_h[...], top_l[...], NN)
        for p in range(N_ROW):
            send3[b, p] = part[:, p * TILE : (p + 1) * TILE].reshape(N_COL, BLOCK, TILE)
        me = own["top"]
        for dz, dx in row_offsets:
            r = rows_at[dz, dx]
            for d in (2, 3, 1, 0):
                q = lax.rem(col + d, N_COL)
                copy = remote(
                    send3.at[b, r, q], got3.at[b, me], rs_out.at[2, b], rs_sem.at[2, b], (col, r, q)
                )
                if (dz, dx, d) != (0, 0, 0):
                    copy.start()
                else:

                    @pl.when(on_diagonal)
                    def _():
                        pltpu.make_async_copy(send3.at[b, r, q], got3.at[b, me], rs_sem.at[2, b]).start()

                    @pl.when(jnp.logical_not(on_diagonal))
                    def _():
                        copy.start()

    gather_far(len(pieces))
    forward_part(0)
    forward_part(1)
    for b in every:
        whole(got3.at[b], rs_sem.at[2, b]).wait()
        spread(2, b, "top", jnp.sum(got3[b], axis=0), s_top)
    for b in every:
        send_result(0, b, batch(s_top, b).at[own["top"]], o_top)
    gathered_all(0)
    prepare_tiles(tm, tm_h, tm_l)
    gathered_all(1)
    prepare(im, mid_h, mid_l)
    for i in range(2):
        whole((all_low, all_mid)[i].at[pl.ds(0, N_COL - 1)], place_sem.at[i]).wait()
    forward_part(2)
    forward_part(3)
    for b in every:
        get_columns(2, b, "top", s_top)
        value = own_columns(mid_y, b) - lower(s_top, b, all_mid, tm_h, tm_l, 16)
        backward(value, b, mid_h, mid_l, send4)
        send_shares(3, b, "mid", send4, got4)
    gathered_all(2)
    prepare_tiles(tl, tl_h, tl_l)
    for b in every:
        spread(3, b, "mid", sum_shares(3, b, "mid", got4), s_mid)
    for b in every:
        send_result(1, b, batch(s_mid, b).at[own["mid"]], o_mid)
    gathered_all(3)
    prepare(il, low_h, low_l)
    for b in every:
        get_columns(3, b, "mid", s_mid)
        value = own_columns(low_y, b) - lower(s_mid, b, all_low, tl_h, tl_l, 8)
        backward(value, b, low_h, low_l, send5)
        send_shares(4, b, "low", send5, got5)
    for b in every:
        tail5[b] = sum_shares(4, b, "low", got5)
        send_result(2, b, tail5.at[b], o_low)

    results = [(o_top, out_top), (o_mid, out_mid), (o_low, out_low)]
    for level, (ref, out) in enumerate(results):
        for b in every:
            whole(ref.at[pl.ds(0, (N_COL - 1) * BLOCK)], res_sem.at[level, b]).wait()
        out[...] = ref[...]

    for b in every:

        @pl.when(is_source)
        def _():
            for _ in group["low"]:
                whole(rl_cut.at[b], start_out.at[b]).wait()

        for level, (ref, _) in enumerate(results):
            whole(ref.at[pl.ds(0, (N_COL - 1) * BLOCK)], res_out.at[level, b]).wait()
        for stage, (kind, send, ref) in enumerate(
            [
                ("mid", send1, x_mid),
                ("top", send2, x_top),
                ("top", None, s_top),
                ("mid", send4, s_mid),
                ("low", send5, None),
            ]
        ):
            count = len(group[kind])
            if send is not None:
                whole(send.at[b, pl.ds(0, count)], rs_out.at[stage, b]).wait()
            if ref is not None:
                whole(batch(ref, b).at[pl.ds(0, count)], ag_out.at[stage, b]).wait()
        whole(got3.at[b, pl.ds(0, TOP - 1)], rs_out.at[2, b]).wait()

        @pl.when(jnp.logical_not(on_diagonal))
        def _():
            whole(got3.at[b, 0], rs_out.at[2, b]).wait()

        for stage in range(3):
            whole(col_got.at[stage, b, pl.ds(0, N_COL - 1)], col_out.at[stage, b]).wait()
    for i, (_, dst) in enumerate(gathered):
        for sem in (far_out, near_out, pass_out):
            whole(dst.at[0], sem.at[i]).wait()
    for i in range(2):
        whole((all_low, all_mid)[i].at[pl.ds(0, N_COL - 1)], place_out.at[i]).wait()


def body(rhs_top, rhs_mid, rhs_low, *others):
    vm = pltpu.VMEM
    wide = N_COL * BLOCK

    def blocks(count):
        return vm((BATCHES, count, BLOCK, TILE), f32)

    def alone(count):
        return [vm((count, BLOCK, TILE), f32)] * BATCHES

    def halves(*shape):
        return [vm(shape, bf16)] * 2

    scratch = [vm((64, TILE), f32)] * 3 + [vm((BATCHES, wide, TILE), f32)] * 3
    scratch += [vm((TILE, 2048), f32)]
    scratch += [vm((N_COL, TILE, size), f32) for size in (1024, 512)]
    scratch += [vm((N_COL, count, TILE, TILE), f32) for count in (4, 2)]
    scratch += [pltpu.SMEM((N_COL, 1, 1, 1, count), jnp.int32) for count in (4, 2)]
    scratch += halves(TILE, 2048) + halves(TILE, 4096) + halves(TILE, 2048) + halves(TILE, 1024) + halves(TILE, 512)
    for count in (16, 8, 4, 2):
        scratch += halves(count * TILE, TILE)
    scratch += [vm((BATCHES, 4, wide, TILE), f32)]
    scratch += [blocks(MID)] * 3 + [blocks(TOP)] * 3 + [vm((BATCHES, N_ROW, N_COL, BLOCK, TILE), f32)]
    scratch += [blocks(TOP)] + alone(TOP) + [blocks(MID)] * 2 + alone(MID)
    scratch += [blocks(LOW)] * 2 + [vm((BATCHES, BLOCK, TILE), f32)]
    scratch += [vm((3, BATCHES, N_COL, wide, TILE), f32)] + [vm((BATCHES, wide, TILE), f32)] * 2
    scratch += [vm((64, TILE), f32)] * 3
    dma = pltpu.SemaphoreType.DMA
    scratch += [dma((8,)), dma((2,)), dma((2,)), dma((BATCHES,)), dma((BATCHES,))]
    scratch += [dma((5, BATCHES)), dma((5, BATCHES)), dma((4, BATCHES)), dma((4, BATCHES))]
    scratch += [dma((3, BATCHES)), dma((3, BATCHES)), dma((3, BATCHES)), dma((3, BATCHES))]
    scratch += [dma((4,))] * 6
    anywhere = pl.BlockSpec(memory_space=pltpu.HBM)
    scalars = pl.BlockSpec(memory_space=pltpu.SMEM)
    out = pl.BlockSpec(memory_space=pltpu.VMEM)
    solved = pl.pallas_call(
        kernel,
        name="solve",
        out_shape=[jax.ShapeDtypeStruct((64, TILE), f32)] * 3,
        in_specs=[anywhere] * 7 + [scalars, anywhere, scalars],
        out_specs=[out] * 3,
        scratch_shapes=scratch,
        compiler_params=pltpu.CompilerParams(
            collective_id=0, has_side_effects=True, vmem_limit_bytes=60 * 1024 * 1024
        ),
    )(rhs_top.T, rhs_mid.T, rhs_low.T, *others)
    return tuple(part.T for part in solved)


def solution(mesh):
    vector = P(("leaf", "row"), None)
    matrix = P(("leaf", "row"), "col")
    tiles = P("leaf", "row", "col", None, None, None)
    places = P("leaf", "row", "col", None)
    return jax.shard_map(
        body,
        mesh=mesh,
        in_specs=(vector, vector, vector, matrix, matrix, matrix, tiles, places, tiles, places),
        out_specs=(vector, vector, vector),
        check_vma=False,
    )
```

```python
import jax
import jax.numpy as jnp
from jax import lax
from jax.experimental import pallas as pl
from jax.experimental.pallas import tpu as pltpu
from jax.sharding import PartitionSpec as P

MESH = pl.DeviceIdType.MESH
TILE = 128
BATCHES = 2
N_LEAF, N_Z, N_X, N_COL = 4, 8, 2, 4
N_ROW = N_Z * N_X
SHARE = 64 // N_COL
BLOCK = SHARE // BATCHES
bf16 = jnp.bfloat16
f32 = jnp.float32
TOP, MID, LOW = 64, 32, 16
PIECES = 2
NN = (((1,), (0,)), ((), ()))
NT = (((1,), (1,)), ((), ()))


def outward(count):
    middle = count // 2
    return [(middle + (-1 if j % 2 else 1) * ((j + 1) // 2)) % count for j in range(count)]


def split(a):
    high = a.astype(bf16)
    return high, (a - high.astype(f32)).astype(bf16)


def product(a, high, low, dims):
    width = a.shape[0]
    a_high = a.astype(bf16).astype(f32)
    both = jnp.concatenate([a_high, a - a_high], axis=0).astype(bf16)
    one = lax.dot_general(both, high, dims, preferred_element_type=f32)
    two = lax.dot_general(both, low, dims, preferred_element_type=f32)
    return (one[:width] + one[width:]) + (two[:width] + two[width:])


def kernel(
    rhs_top, rhs_mid, rhs_low, inv_top, inv_mid, inv_low, tiles_mid, places_mid, tiles_low, places_low,
    out_top, out_mid, out_low,
    rt, rm, rl, rt_cut, rm_cut, rl_cut,
    it, im, il, tm, tl, all_mid, all_low,
    top_h, top_l, mid_h, mid_l, low_h, low_l, own_mid_h, own_mid_l, own_low_h, own_low_l,
    tm_h, tm_l, tl_h, tl_l, own_tm_h, own_tm_l, own_tl_h, own_tl_l,
    x_low, send1, got1, x_mid, send2, got2, x_top, send3, got3, s_top_0, s_top_1, send4, got4, s_mid_0, s_mid_1,
    send5, got5, tail5, col_got, low_y, mid_y, o_top, o_mid, o_low,
    load_sem, place_sem, place_out, start_sem, start_out, rs_sem, rs_out, ag_sem, ag_out, col_sem, col_out,
    res_sem, res_out, far_sem, far_out, near_sem, near_out, pass_sem, pass_out,
):
    leaf = lax.axis_index("leaf")
    row = lax.axis_index("row")
    col = lax.axis_index("col")
    z = row // N_X
    x = lax.rem(row, N_X)
    pair = leaf // 2 * 2
    every = range(BATCHES)
    wide = N_COL * BLOCK
    s_top, s_mid = (s_top_0, s_top_1), (s_mid_0, s_mid_1)

    rows_at = {}
    for dz in range(N_Z):
        for dx in range(N_X):
            rows_at[dz, dx] = lax.rem(z + dz, N_Z) * N_X + lax.rem(x + dx, N_X)
    row_offsets = [(dz, dx) for dz in outward(N_Z) for dx in (1, 0)]

    def peers(kind):
        if kind == "top":
            leaves = [(lax.rem(leaf + dy, N_LEAF), dy) for dy in outward(N_LEAF)]
        elif kind == "mid":
            leaves = [(pair + lax.rem(leaf - pair + dy, 2), dy) for dy in (1, 0)]
        else:
            leaves = [(leaf, 0)]
        found = []
        for other, dy in leaves:
            for dz, dx in row_offsets:
                if (dy, dz, dx) != (0, 0, 0):
                    r = rows_at[dz, dx]
                    base = {"top": other, "mid": other - pair, "low": 0}[kind]
                    found.append((base * N_ROW + r, (other, r, col)))
        return found

    group = {k: peers(k) for k in ("top", "mid", "low")}
    own = {"top": leaf * N_ROW + row, "mid": (leaf - pair) * N_ROW + row, "low": row}
    other_cols = [lax.rem(col + d, N_COL) for d in (2, 3, 1)]
    others = [(leaf, row, c) for c in other_cols]
    far_col = lax.rem(col + 2, N_COL)
    near_col = col + 1 - 2 * lax.rem(col, 2)
    far, near = (leaf, row, far_col), (leaf, row, near_col)
    on_diagonal = leaf == col
    below = leaf >= col

    def remote(src, dst, send, recv, device):
        return pltpu.make_async_remote_copy(
            src_ref=src, dst_ref=dst, send_sem=send, recv_sem=recv, device_id=device, device_id_type=MESH
        )

    def whole(ref, sem):
        return pltpu.make_async_copy(ref, ref, sem)

    def batch(ref, b):
        return ref[b] if isinstance(ref, tuple) else ref.at[b]

    gathered = [
        (tiles_mid.at[0, 0, 0], tm),
        (inv_mid, im),
        (tiles_low.at[0, 0, 0], tl),
        (inv_low, il),
    ]
    places_of = [(inv_low, il.at[col]), (tiles_low.at[0, 0, 0], tl.at[col]), (inv_mid, im.at[col])]
    places_of += [(tiles_mid.at[0, 0, 0], tm.at[col]), (inv_top, it)]
    copies = [(rhs_low, rl), places_of[0], places_of[1], (rhs_mid, rm), places_of[2], places_of[3], (rhs_top, rt)]
    copies += [places_of[4]]
    loads = [pltpu.make_async_copy(src, dst, load_sem.at[i]) for i, (src, dst) in enumerate(copies)]
    for load in loads:
        load.start()

    for ref in (got3, got4, got5):
        ref[...] = jnp.zeros_like(ref)

    barrier = pltpu.get_barrier_semaphore()
    for _, device in group["top"]:
        pl.semaphore_signal(barrier, inc=1, device_id=device, device_id_type=MESH)
    for device in others:
        pl.semaphore_signal(barrier, inc=1, device_id=device, device_id_type=MESH)
    for dy in outward(N_LEAF):
        for dz, dx in row_offsets:
            source = (lax.rem(leaf + dy, N_LEAF), rows_at[dz, dx], leaf)
            if (dy, dz, dx) != (0, 0, 0):
                pl.semaphore_signal(barrier, inc=1, device_id=source, device_id_type=MESH)
            else:

                @pl.when(jnp.logical_not(on_diagonal))
                def _():
                    pl.semaphore_signal(barrier, inc=1, device_id=source, device_id_type=MESH)

    def cut_batches(ref, to):
        for b in every:
            for q in range(N_COL):
                to[b, q * BLOCK : (q + 1) * BLOCK] = ref[q * SHARE + b * BLOCK : q * SHARE + (b + 1) * BLOCK]

    loads[0].wait()
    cut_batches(rl, rl_cut)
    pl.semaphore_wait(barrier, len(group["top"]) + len(others) + TOP - on_diagonal.astype(jnp.int32))

    is_source = col == row // 4
    place_low = lax.rem(row, 4)

    @pl.when(is_source)
    def _():
        for b in every:
            here = x_low.at[b, place_low]
            for _, device in group["low"]:
                remote(rl_cut.at[b], here, start_out.at[b], start_sem.at[b], device).start()
            pltpu.make_async_copy(rl_cut.at[b], here, start_sem.at[b]).start()

    pieces = []
    for i, count in ((0, 4), (1, 8), (2, 2), (3, 4)):
        step = gathered[i][0].shape[0] // count
        pieces += [(i, pl.ds(n * step, step)) for n in range(count)]
    pieces.reverse()

    def gather_far(count=PIECES):
        for _ in range(min(count, len(pieces))):
            i, cut = pieces.pop()
            src, dst = gathered[i]
            remote(src.at[cut], dst.at[col, cut], far_out.at[i], far_sem.at[i], far).start()

    def forward_part(i):
        dst = gathered[i][1].at[far_col]
        whole(dst, far_sem.at[i]).wait()
        remote(dst, dst, pass_out.at[i], pass_sem.at[i], near).start()

    def gathered_all(i):
        part = gathered[i][1].at[0]
        whole(part, near_sem.at[i]).wait()
        whole(part, pass_sem.at[i]).wait()

    for (src, dst), sem, out in ((places_low, all_low), place_sem.at[0], place_out.at[0]), (
        (places_mid, all_mid), place_sem.at[1], place_out.at[1]
    ):
        for device in others:
            remote(src, dst.at[col], out, sem, device).start()
        for n in range(src.shape[3]):
            dst[col, 0, 0, 0, n] = src[0, 0, 0, n]
    for i, (src, dst) in enumerate(gathered):
        remote(src, dst.at[col], near_out.at[i], near_sem.at[i], near).start()
    gather_far()

    def prepare(raw, high, low):
        size = raw.shape[2]
        for c in range(N_COL):
            for p in range(0, size, 512):
                cut = slice(c * size + p, c * size + p + 512)
                high[:, cut], low[:, cut] = split(raw[c, :, p : p + 512])

    def prepare_own(raw, high, low):
        for p in range(0, high.shape[1], 512):
            cut = slice(p, p + 512)
            high[:, cut], low[:, cut] = split(raw[:, cut])

    def prepare_tiles(raw, high, low):
        count = raw.shape[1]
        for c in range(N_COL):
            for n in range(count):
                cut = slice((c * count + n) * TILE, (c * count + n + 1) * TILE)
                high[cut], low[cut] = split(raw[c, n])

    def prepare_own_tiles(raw, high, low):
        for n in range(raw.shape[1]):
            cut = slice(n * TILE, (n + 1) * TILE)
            high[cut], low[cut] = split(raw[col, n])

    loads[1].wait()
    prepare_own(il.at[col], own_low_h, own_low_l)

    def send_shares(stage, b, kind, send, got):
        me = own[kind]
        for k, device in group[kind]:
            remote(send.at[b, k], got.at[b, me], rs_out.at[stage, b], rs_sem.at[stage, b], device).start()
        got[b, me] = send[b, me]

    def sum_shares(stage, b, kind, got):
        whole(got.at[b, pl.ds(0, len(group[kind]))], rs_sem.at[stage, b]).wait()
        return jnp.sum(got[b], axis=0)

    def spread(stage, b, kind, total, ref):
        mine = batch(ref, b).at[own[kind]]
        mine[...] = total
        if stage != 1:
            for _, device in group[kind]:
                remote(mine, mine, ag_out.at[stage, b], ag_sem.at[stage, b], device).start()
            return
        for other, devices in leaf_groups():

            @pl.when(other >= col)
            def _():
                for device in devices:
                    remote(mine, mine, ag_out.at[stage, b], ag_sem.at[stage, b], device).start()

    def leaf_groups():
        devices = [device for _, device in group["top"]]
        return [(devices[at][0], devices[at : at + N_ROW]) for at in range(0, TOP, N_ROW)]

    def get_columns(stage, b, kind, ref):
        whole(batch(ref, b).at[pl.ds(0, len(group[kind]))], ag_sem.at[stage, b]).wait()

    def send_col(stage, b, value):
        mine = col_got.at[stage, b, col]
        mine[...] = value
        for device in others:
            remote(mine, mine, col_out.at[stage, b], col_sem.at[stage, b], device).start()

    def get_col(stage, b):
        whole(col_got.at[stage, b, pl.ds(0, N_COL - 1)], col_sem.at[stage, b]).wait()
        got = [col_got[stage, b, c] for c in range(N_COL)]
        return (got[0] + got[1]) + (got[2] + got[3])

    def forward(ref, b, positions, high, low):
        columns = jnp.concatenate(
            [ref[b, p * N_COL : (p + 1) * N_COL].reshape(wide, TILE) for p in range(positions)], axis=1
        )
        return product(columns, high[...], low[...], NT)

    def lift(vector, b, places, high, low, rhs, is_mine, my_place, send, positions):
        count = places.shape[3]
        parts = product(vector, high[...], low[...], NT)
        mine = jnp.where(is_mine, rhs[b], 0.0)
        for p in range(positions):
            value = jnp.where(my_place == p, mine, 0.0)
            for n in range(count):
                value = value - jnp.where(places[0, 0, 0, n] == p, parts[:, n * TILE : (n + 1) * TILE], 0.0)
            send[b, p * N_COL : (p + 1) * N_COL] = value.reshape(N_COL, BLOCK, TILE)

    def lower(ref, b, places, high, low, positions):
        count = places.shape[4]
        picked = [
            batch(ref, b)[c * positions + places[c, 0, 0, 0, n]] for c in range(N_COL) for n in range(count)
        ]
        return product(jnp.concatenate(picked, axis=1), high[...], low[...], NN)

    def backward(value, b, high, low, send):
        part = product(value, high[...], low[...], NN)
        for p in range(high.shape[1] // TILE):
            send[b, p] = part[:, p * TILE : (p + 1) * TILE]

    def own_columns(ref, b):
        return ref[b, pl.ds(pl.multiple_of(col * BLOCK, BLOCK), BLOCK)]

    def send_result(level, b, src, out):
        place = pl.ds(pl.multiple_of(col * SHARE + b * BLOCK, BLOCK), BLOCK)
        for device in others:
            remote(src, out.at[place], res_out.at[level, b], res_sem.at[level, b], device).start()
        out[place] = src[...]

    mid_index = own["mid"]
    mine_mid, place_mid = col == mid_index // 8, lax.rem(mid_index, 8)

    for b in every:
        whole(x_low.at[b], start_sem.at[b]).wait()
        columns = jnp.concatenate([x_low[b, p] for p in range(4)], axis=1)
        send_col(0, b, product(columns, own_low_h[...], own_low_l[...], NT))
    gather_far()
    loads[2].wait()
    prepare_own_tiles(tl, own_tl_h, own_tl_l)
    loads[3].wait()
    cut_batches(rm, rm_cut)
    for b in every:
        low_y[b] = get_col(0, b)
        lift(low_y[b], b, places_low, own_tl_h, own_tl_l, rm_cut, mine_mid, place_mid, send1, 8)
        send_shares(0, b, "mid", send1, got1)
    gather_far()
    loads[4].wait()
    prepare_own(im.at[col], own_mid_h, own_mid_l)
    for b in every:
        spread(0, b, "mid", sum_shares(0, b, "mid", got1), x_mid)
    gather_far()
    loads[5].wait()
    prepare_own_tiles(tm, own_tm_h, own_tm_l)
    loads[6].wait()
    cut_batches(rt, rt_cut)
    for b in every:
        get_columns(0, b, "mid", x_mid)
        send_col(1, b, forward(x_mid, b, 8, own_mid_h, own_mid_l))
    gather_far()
    for b in every:
        mid_y[b] = get_col(1, b)
        lift(mid_y[b], b, places_mid, own_tm_h, own_tm_l, rt_cut, on_diagonal, row, send2, 16)
        send_shares(1, b, "top", send2, got2)
    gather_far()
    loads[7].wait()
    prepare_own(it, top_h, top_l)
    for b in every:
        spread(1, b, "top", sum_shares(1, b, "top", got2), x_top)
    gather_far()
    for b in every:
        mine = col_got.at[2, b, col]

        @pl.when(below)
        def _():
            get_columns(1, b, "top", x_top)
            mine[...] = forward(x_top, b, 16, top_h, top_l)

        @pl.when(jnp.logical_not(below))
        def _():
            mine[...] = jnp.zeros_like(mine)

        for device in others:
            remote(mine, mine, col_out.at[2, b], col_sem.at[2, b], device).start()
    gather_far()
    for b in every:
        top_y = get_col(2, b)

        @pl.when(below)
        def _():
            part = product(top_y, top_h[...], top_l[...], NN)
            for p in range(N_ROW):
                send3[b, p] = part[:, p * TILE : (p + 1) * TILE].reshape(N_COL, BLOCK, TILE)
            me = own["top"]
            for dz, dx in row_offsets:
                r = rows_at[dz, dx]
                for d in (2, 3, 1, 0):
                    q = lax.rem(col + d, N_COL)
                    copy = remote(
                        send3.at[b, r, q], got3.at[b, me], rs_out.at[2, b], rs_sem.at[2, b], (col, r, q)
                    )
                    if (dz, dx, d) != (0, 0, 0):
                        copy.start()
                    else:

                        @pl.when(on_diagonal)
                        def _():
                            pltpu.make_async_copy(send3.at[b, r, q], got3.at[b, me], rs_sem.at[2, b]).start()

                        @pl.when(jnp.logical_not(on_diagonal))
                        def _():
                            copy.start()

    gather_far(len(pieces))
    forward_part(0)
    forward_part(1)
    for b in every:
        for leaves in range(1, N_LEAF + 1):

            @pl.when(N_LEAF - leaf == leaves)
            def _():
                whole(got3.at[b, pl.ds(0, leaves * N_ROW)], rs_sem.at[2, b]).wait()

        spread(2, b, "top", jnp.sum(got3[b], axis=0), s_top)
    for b in every:
        send_result(0, b, batch(s_top, b).at[own["top"]], o_top)
    gathered_all(0)
    prepare_tiles(tm, tm_h, tm_l)
    gathered_all(1)
    prepare(im, mid_h, mid_l)
    for i in range(2):
        whole((all_low, all_mid)[i].at[pl.ds(0, N_COL - 1)], place_sem.at[i]).wait()
    forward_part(2)
    forward_part(3)
    for b in every:
        get_columns(2, b, "top", s_top)
        value = own_columns(mid_y, b) - lower(s_top, b, all_mid, tm_h, tm_l, 16)
        backward(value, b, mid_h, mid_l, send4)
        send_shares(3, b, "mid", send4, got4)
    gathered_all(2)
    prepare_tiles(tl, tl_h, tl_l)
    for b in every:
        spread(3, b, "mid", sum_shares(3, b, "mid", got4), s_mid)
    for b in every:
        send_result(1, b, batch(s_mid, b).at[own["mid"]], o_mid)
    gathered_all(3)
    prepare(il, low_h, low_l)
    for b in every:
        get_columns(3, b, "mid", s_mid)
        value = own_columns(low_y, b) - lower(s_mid, b, all_low, tl_h, tl_l, 8)
        backward(value, b, low_h, low_l, send5)
        send_shares(4, b, "low", send5, got5)
    for b in every:
        tail5[b] = sum_shares(4, b, "low", got5)
        send_result(2, b, tail5.at[b], o_low)

    results = [(o_top, out_top), (o_mid, out_mid), (o_low, out_low)]
    for level, (ref, out) in enumerate(results):
        for b in every:
            whole(ref.at[pl.ds(0, (N_COL - 1) * BLOCK)], res_sem.at[level, b]).wait()
        out[...] = ref[...]

    for b in every:

        @pl.when(is_source)
        def _():
            for _ in group["low"]:
                whole(rl_cut.at[b], start_out.at[b]).wait()

        for level, (ref, _) in enumerate(results):
            whole(ref.at[pl.ds(0, (N_COL - 1) * BLOCK)], res_out.at[level, b]).wait()
        for stage, (kind, send, ref) in enumerate(
            [
                ("mid", send1, x_mid),
                ("top", send2, None),
                ("top", None, s_top),
                ("mid", send4, s_mid),
                ("low", send5, None),
            ]
        ):
            count = len(group[kind])
            if send is not None:
                whole(send.at[b, pl.ds(0, count)], rs_out.at[stage, b]).wait()
            if ref is not None:
                whole(batch(ref, b).at[pl.ds(0, count)], ag_out.at[stage, b]).wait()

        @pl.when(on_diagonal)
        def _():
            whole(got3.at[b, pl.ds(0, TOP - 1)], rs_out.at[2, b]).wait()

        @pl.when(leaf > col)
        def _():
            whole(got3.at[b], rs_out.at[2, b]).wait()

        for leaves in range(1, N_LEAF + 1):
            for mine in (0, 1):
                sent = leaves * N_ROW - mine

                @pl.when(jnp.logical_and(N_LEAF - col == leaves, below if mine else jnp.logical_not(below)))
                def _():
                    whole(x_top.at[b, pl.ds(0, sent)], ag_out.at[1, b]).wait()

        for stage in range(3):
            whole(col_got.at[stage, b, pl.ds(0, N_COL - 1)], col_out.at[stage, b]).wait()
    for i, (_, dst) in enumerate(gathered):
        for sem in (far_out, near_out, pass_out):
            whole(dst.at[0], sem.at[i]).wait()
    for i in range(2):
        whole((all_low, all_mid)[i].at[pl.ds(0, N_COL - 1)], place_out.at[i]).wait()


def body(rhs_top, rhs_mid, rhs_low, *others):
    vm = pltpu.VMEM
    wide = N_COL * BLOCK

    def blocks(count):
        return vm((BATCHES, count, BLOCK, TILE), f32)

    def alone(count):
        return [vm((count, BLOCK, TILE), f32)] * BATCHES

    def halves(*shape):
        return [vm(shape, bf16)] * 2

    scratch = [vm((64, TILE), f32)] * 3 + [vm((BATCHES, wide, TILE), f32)] * 3
    scratch += [vm((TILE, 2048), f32)]
    scratch += [vm((N_COL, TILE, size), f32) for size in (1024, 512)]
    scratch += [vm((N_COL, count, TILE, TILE), f32) for count in (4, 2)]
    scratch += [pltpu.SMEM((N_COL, 1, 1, 1, count), jnp.int32) for count in (4, 2)]
    scratch += halves(TILE, 2048) + halves(TILE, 4096) + halves(TILE, 2048) + halves(TILE, 1024) + halves(TILE, 512)
    for count in (16, 8, 4, 2):
        scratch += halves(count * TILE, TILE)
    scratch += [vm((BATCHES, 4, wide, TILE), f32)]
    scratch += [blocks(MID)] * 3 + [blocks(TOP)] * 3 + [vm((BATCHES, N_ROW, N_COL, BLOCK, TILE), f32)]
    scratch += [blocks(TOP)] + alone(TOP) + [blocks(MID)] * 2 + alone(MID)
    scratch += [blocks(LOW)] * 2 + [vm((BATCHES, BLOCK, TILE), f32)]
    scratch += [vm((3, BATCHES, N_COL, wide, TILE), f32)] + [vm((BATCHES, wide, TILE), f32)] * 2
    scratch += [vm((64, TILE), f32)] * 3
    dma = pltpu.SemaphoreType.DMA
    scratch += [dma((8,)), dma((2,)), dma((2,)), dma((BATCHES,)), dma((BATCHES,))]
    scratch += [dma((5, BATCHES)), dma((5, BATCHES)), dma((4, BATCHES)), dma((4, BATCHES))]
    scratch += [dma((3, BATCHES)), dma((3, BATCHES)), dma((3, BATCHES)), dma((3, BATCHES))]
    scratch += [dma((4,))] * 6
    anywhere = pl.BlockSpec(memory_space=pltpu.HBM)
    scalars = pl.BlockSpec(memory_space=pltpu.SMEM)
    out = pl.BlockSpec(memory_space=pltpu.VMEM)
    solved = pl.pallas_call(
        kernel,
        name="solve",
        out_shape=[jax.ShapeDtypeStruct((64, TILE), f32)] * 3,
        in_specs=[anywhere] * 7 + [scalars, anywhere, scalars],
        out_specs=[out] * 3,
        scratch_shapes=scratch,
        compiler_params=pltpu.CompilerParams(
            collective_id=0, has_side_effects=True, vmem_limit_bytes=60 * 1024 * 1024
        ),
    )(rhs_top.T, rhs_mid.T, rhs_low.T, *others)
    return tuple(part.T for part in solved)


def solution(mesh):
    vector = P(("leaf", "row"), None)
    matrix = P(("leaf", "row"), "col")
    tiles = P("leaf", "row", "col", None, None, None)
    places = P("leaf", "row", "col", None)
    return jax.shard_map(
        body,
        mesh=mesh,
        in_specs=(vector, vector, vector, matrix, matrix, matrix, tiles, places, tiles, places),
        out_specs=(vector, vector, vector),
        check_vma=False,
    )
```
